32 devices in a mesh: row: 2 (over core), col: 8 (over z, x), layer: 2 (over y).
Axes of the slice: x: 2, y: 2, z: 4, core: 2. Of those that a mesh axis runs over, the one named last changes fastest.
Arguments:
- tile_values: float32 [2, 16, 2, 6, 128, 128], P('row', ('col', 'layer')), may hold values from -1.8 to 1.8
- tile_rows: int32 [2, 16, 2, 6], P('row', ('col', 'layer')), may hold values from 0 to 127, as said below
- tile_cols: int32 [2, 16, 2, 6], P('row', ('col', 'layer')), may hold values from 0 to 127, as said below
- tile_counts: int32 [2, 16, 2], P('row', ('col', 'layer')), may hold values from 1 to 6, as said below
- out_rows: int32 [2, 8, 2, 12], P('row', 'col'), may hold values from 0 to 127, as said below
- out_cols: int32 [2, 8, 2, 12], P('row', 'col'), may hold values from 0 to 127, as said below
Outputs:
- squared: float32 [2, 16, 12, 128, 128], P('row', ('col', 'layer'))
The draws below stay inside these ranges and needn't reach their ends.
Inputs may be any that keep to these rules, and one draw needn't show every extreme that they name: `tile_rows`: entry [r, s, h, q] lies in row band r (the 64 block rows from r * 64), in a run of 8 block rows whose index is congruent to h modulo 2; within one list [r, s, h] the 6 slots have distinct rows. `tile_cols`: entry [r, s, h, q] lies in sub-band s: block columns s * 8 to s * 8 + 7. Slots q < tile_counts[r, s, h] of list [r, s, h] hold tiles; values and coordinates in later slots mean nothing. Some list holds 6 tiles in every draw. out_rows[r, c, l, o] and out_cols[r, c, l, o] place the o-th kept tile of row band r and sub-band c * 2 + l; the row lies in row band r, the column in that sub-band, and the 12 positions of one [r, c, l] are distinct. `out_cols`: see out_rows.
All inputs are finite; a program needn't handle non-finite values.
Results may differ from the reference program's by a relative error of at most 0.0003.
Values sent between devices are 32-bit elements; how exact they have to be, the bound alone decides.
A program may use at most 128 MiB of HBM per device.

```python
import jax
import jax.numpy as jnp
from jax import lax

BS = 128
NBS = 8
CAP = 6
OCAP = 12
N_ROW = 2
N_COL = 8
N_LAYER = 2


def layout(key):
    sub_count = N_COL * N_LAYER
    block_count = NBS * sub_count
    band_rows = block_count // N_ROW
    half_rows = band_rows // N_LAYER
    list_shape = (N_ROW, sub_count, N_LAYER)
    list_total = N_ROW * sub_count * N_LAYER
    counts = jax.random.randint(jax.random.fold_in(key, 101), list_shape, 1, CAP + 1)
    chosen = jax.random.randint(jax.random.fold_in(key, 102), (), 0, list_total)
    counts = jnp.where(jnp.arange(list_total).reshape(list_shape) == chosen, CAP, counts).astype(jnp.int32)
    row_scores = jax.random.randint(jax.random.fold_in(key, 103), list_shape + (half_rows,), 0, 4096) * half_rows + jnp.arange(half_rows)
    unused, local_rows = lax.top_k(row_scores, CAP)
    band_block = local_rows // NBS * N_LAYER + jnp.arange(N_LAYER)[None, None, :, None]
    rows = jnp.arange(N_ROW)[:, None, None, None] * band_rows + band_block * NBS + local_rows % NBS
    rows = rows.astype(jnp.int32)
    cols = jnp.arange(sub_count)[None, :, None, None] * NBS + jax.random.randint(jax.random.fold_in(key, 104), list_shape + (CAP,), 0, NBS)
    cols = cols.astype(jnp.int32)
    live_mask = jnp.arange(CAP)[None, None, None, :] < counts[..., None]
    live_rows = jnp.where(live_mask, rows, block_count).reshape(-1)
    occupancy = jnp.zeros((block_count + 1, block_count), jnp.int32).at[live_rows, cols.reshape(-1)].set(1)[:block_count]
    reach = jnp.minimum(jnp.dot(occupancy, occupancy), 1)
    spots = band_rows * NBS
    reach_blocks = reach.reshape(N_ROW, band_rows, sub_count, NBS).transpose(0, 2, 1, 3).reshape(N_ROW, sub_count, spots)
    out_scores = reach_blocks * (1 << 28) + jax.random.randint(jax.random.fold_in(key, 105), (N_ROW, sub_count, spots), 0, 256) * spots + jnp.arange(spots)
    unused_too, picked = lax.top_k(out_scores, OCAP)
    kept_rows = jnp.arange(N_ROW)[:, None, None] * band_rows + picked // NBS
    kept_cols = jnp.arange(sub_count)[None, :, None] * NBS + picked % NBS
    kept_rows = kept_rows.reshape(N_ROW, N_COL, N_LAYER, OCAP).astype(jnp.int32)
    kept_cols = kept_cols.reshape(N_ROW, N_COL, N_LAYER, OCAP).astype(jnp.int32)
    return (rows, cols, counts, kept_rows, kept_cols)


def draw_tile_rows(key, part):
    return layout(key)[0]


def draw_tile_cols(key, part):
    return layout(key)[1]


def draw_tile_counts(key, part):
    return layout(key)[2]


def draw_out_rows(key, part):
    return layout(key)[3]


def draw_out_cols(key, part):
    return layout(key)[4]


def block_levels(own_key, shape, split, smallest, high):
    level = 1.0
    for axis_at, blocks in split:
        draws = jax.random.uniform(jax.random.fold_in(jax.random.fold_in(own_key, 6), axis_at), (blocks,), jnp.float32, smallest / len(split), high / len(split))
        level = level * jnp.repeat(jnp.exp(draws), shape[axis_at] // blocks).reshape((-1,) + (1,) * (len(shape) - 1 - axis_at))
    return level


def noise(own_key, shape, width, bound, cuts=(), kind=jnp.bfloat16):
    values = width * jax.random.normal(own_key, shape, jnp.float32)
    if cuts:
        values = values * block_levels(own_key, shape, cuts, -0.22, 0.18)
    return jnp.clip(values, -bound, bound).astype(kind)


def setup_inputs(seed: int = 0) -> dict:
    splits = jax.random.split(jax.random.key(seed), 7)
    tile_values = noise(splits[0], (N_ROW, N_COL * N_LAYER, N_LAYER, CAP, BS, BS), 0.3, 1.8, ((0, 2), (1, 16)), jnp.float32)
    tile_rows = draw_tile_rows(jax.random.fold_in(splits[6], 71), 0)
    tile_cols = draw_tile_cols(jax.random.fold_in(splits[6], 71), 0)
    tile_counts = draw_tile_counts(jax.random.fold_in(splits[6], 71), 0)
    out_rows = draw_out_rows(jax.random.fold_in(splits[6], 71), 0)
    out_cols = draw_out_cols(jax.random.fold_in(splits[6], 71), 0)
    return dict(tile_values=tile_values, tile_rows=tile_rows, tile_cols=tile_cols, tile_counts=tile_counts, out_rows=out_rows, out_cols=out_cols)


def tile_lookup(tile_rows, tile_cols, tile_counts, block_count):
    slot_ids = jnp.arange(CAP, dtype=jnp.int32)
    is_live = slot_ids[None, None, None, :] < tile_counts[..., None]
    live_rows = jnp.where(is_live, tile_rows, block_count).astype(jnp.int32).reshape(-1)
    live_cols = tile_cols.astype(jnp.int32).reshape(-1)
    tile_ids = jnp.arange(live_rows.shape[0], dtype=jnp.int32)
    blank = jnp.full((block_count + 1, block_count), -1, dtype=jnp.int32)
    return blank.at[live_rows, live_cols].set(tile_ids)[:block_count]


def reference(tile_values, tile_rows, tile_cols, tile_counts, out_rows, out_cols):
    sub_count = N_COL * N_LAYER
    block_count = NBS * sub_count
    lookup = tile_lookup(tile_rows, tile_cols, tile_counts, block_count)
    flat_values = tile_values.reshape(-1, BS, BS)
    offsets = jnp.arange(sub_count, dtype=jnp.int32) * NBS

    def one_target(target):
        row_index, col_index = target
        row_table = lookup[row_index].reshape(sub_count, NBS)
        left_ids = jnp.max(row_table, axis=1)
        inner_index = jnp.argmax(row_table, axis=1).astype(jnp.int32) + offsets
        right_ids = lookup[inner_index, col_index]
        weight = jnp.where((left_ids >= 0) & (right_ids >= 0), 1.0, 0.0).astype(jnp.float32)
        left_tiles = flat_values[jnp.maximum(left_ids, 0)]
        right_tiles = flat_values[jnp.maximum(right_ids, 0)]
        products = jnp.einsum("spq,sqr->spr", left_tiles, right_tiles, precision=lax.Precision.HIGHEST)
        return jnp.sum(products * weight[:, None, None], axis=0)

    rows_grouped = out_rows.astype(jnp.int32).reshape(-1, OCAP)
    cols_grouped = out_cols.astype(jnp.int32).reshape(-1, OCAP)
    result = lax.map(jax.vmap(one_target), (rows_grouped, cols_grouped))
    return result.reshape(N_ROW, N_COL * N_LAYER, OCAP, BS, BS)
```

```python
import functools

import jax
import jax.numpy as jnp
from jax import lax
from jax.experimental import pallas as pl
from jax.experimental.pallas import tpu as pltpu
from jax.sharding import PartitionSpec as P

ROUND = 16
MESH = pl.DeviceIdType.MESH


def greet(others):
    barrier = pltpu.get_barrier_semaphore()
    count = len(others) if isinstance(others, list) else others[0]
    if isinstance(others, list):
        for device in others:
            pl.semaphore_signal(barrier, inc=1, device_id=device, device_id_type=MESH)
    else:
        make = others[1]

        def step(k, unused):
            pl.semaphore_signal(barrier, inc=1, device_id=make(k + 1), device_id_type=MESH)
            return unused

        lax.fori_loop(0, count, step, 0)
    pl.semaphore_wait(barrier, count)


def spread_kernel(
    n_row, n_sub, n_layer, tiles, meta, landed, panel, meta_all,
    send_sem, recv_sem, panel_send, panel_recv, meta_send, meta_recv, local_sem,
):
    row = lax.axis_index("row")
    sub = lax.axis_index("col") * n_layer + lax.axis_index("layer")
    total = n_row * n_sub
    flat = row * n_sub + sub

    def device_at(flat_index):
        band, place = flat_index // n_sub, flat_index % n_sub
        return {"row": band, "col": place // n_layer, "layer": place % n_layer}

    def other(k):
        return device_at(lax.rem(flat + k, total))

    greet((total - 1, other))

    def meta_copy(k):
        return pltpu.make_async_remote_copy(
            src_ref=meta, dst_ref=meta_all.at[flat], send_sem=meta_send.at[k],
            recv_sem=meta_recv.at[k], device_id=other(k), device_id_type=MESH)

    def slice_copy(k):
        place = lax.rem(sub + k, n_sub)
        return pltpu.make_async_remote_copy(
            src_ref=tiles.at[:, place], dst_ref=landed.at[sub], send_sem=send_sem.at[k],
            recv_sem=recv_sem.at[k],
            device_id={"row": row, "col": place // n_layer, "layer": place % n_layer},
            device_id_type=MESH)

    def panel_copy(k):
        return pltpu.make_async_remote_copy(
            src_ref=tiles, dst_ref=panel.at[row], send_sem=panel_send.at[k],
            recv_sem=panel_recv.at[k],
            device_id={"row": lax.rem(row + k, n_row), "col": sub // n_layer,
                       "layer": sub % n_layer},
            device_id_type=MESH)

    def each(count, what):
        def step(k, unused):
            what(k + 1)
            return unused
        lax.fori_loop(0, count, step, 0)

    own_meta = pltpu.make_async_copy(meta, meta_all.at[flat], local_sem.at[0])
    own_slice = pltpu.make_async_copy(tiles.at[:, sub], landed.at[sub], local_sem.at[1])
    own_panel = pltpu.make_async_copy(tiles, panel.at[row], local_sem.at[2])
    each(total - 1, lambda k: meta_copy(k).start())
    each(n_sub - 1, lambda k: slice_copy(k).start())
    each(n_row - 1, lambda k: panel_copy(k).start())
    own_meta.start()
    own_slice.start()
    own_panel.start()
    own_meta.wait()
    own_slice.wait()
    own_panel.wait()
    each(total - 1, lambda k: meta_copy(k).wait())
    each(n_row - 1, lambda k: panel_copy(k).wait())
    each(n_sub - 1, lambda k: slice_copy(k).wait())


def deliver_kernel(n_sub, n_layer, wanted, landed, arrived, packed, send_sem, recv_sem, local_sem):
    row = lax.axis_index("row")
    sub = lax.axis_index("col") * n_layer + lax.axis_index("layer")

    def device_of(place):
        return {"row": row, "col": place // n_layer, "layer": place % n_layer}

    greet((n_sub - 1, lambda k: device_of(lax.rem(sub + k, n_sub))))

    def pack(place):
        for n in range(ROUND):
            packed[place, n] = landed[wanted[place, n]]

    def send(k):
        place = lax.rem(sub + k, n_sub)
        return pltpu.make_async_remote_copy(
            src_ref=packed.at[place], dst_ref=arrived.at[:, sub], send_sem=send_sem.at[k],
            recv_sem=recv_sem.at[k], device_id=device_of(place), device_id_type=MESH)

    def out_step(k, unused):
        pack(lax.rem(sub + k + 1, n_sub))
        send(k + 1).start()
        return unused

    def wait_step(k, unused):
        send(k + 1).wait()
        return unused

    lax.fori_loop(0, n_sub - 1, out_step, 0)
    pack(sub)
    own = pltpu.make_async_copy(packed.at[sub], arrived.at[:, sub], local_sem)
    own.start()
    own.wait()
    lax.fori_loop(0, n_sub - 1, wait_step, 0)


def multiply_kernel(base, counts, listed, arrived, panel, out):
    order = out.shape[-1]

    def split(value):
        high = value.astype(jnp.bfloat16)
        return high, (value - high.astype(jnp.float32)).astype(jnp.bfloat16)

    def product(left, right):
        left_high, left_low = split(left)
        right_high, right_low = split(right)
        lefts = jnp.concatenate([left_high, left_high, left_low], axis=1)
        rights = jnp.concatenate([right_high, right_low, right_high], axis=0)
        return jnp.dot(lefts, rights, preferred_element_type=jnp.float32)

    for o in range(out.shape[0]):
        def add(m, unused):
            code = listed[o, m]
            left_index = code // base
            right = panel[code % base]

            @pl.when(left_index < ROUND)
            def _():
                out[o] += product(arrived[left_index], right)

            @pl.when(left_index >= ROUND)
            def _():
                out[o] += product(panel[left_index - ROUND], right)

            return unused

        out[o] = jnp.zeros((order, order), jnp.float32)
        lax.fori_loop(0, counts[o], add, 0)


def running_count(flags):
    size = flags.shape[-1]
    upper = (jnp.arange(size)[:, None] <= jnp.arange(size)[None, :]).astype(jnp.bfloat16)
    return jnp.dot(flags.astype(jnp.bfloat16), upper,
                   preferred_element_type=jnp.float32).astype(jnp.int32)


def local(n_row, n_col, n_layer, tile_values, tile_rows, tile_cols, tile_counts, out_rows, out_cols):
    order = tile_values.shape[-1]
    slots = tile_values.shape[2] * tile_values.shape[3]
    kept = out_rows.shape[-1]
    n_sub = n_col * n_layer
    part = order // n_sub
    total = n_row * n_sub
    row = lax.axis_index("row")
    layer = lax.axis_index("layer")
    sub = lax.axis_index("col") * n_layer + layer

    tiles = tile_values.reshape(slots, n_sub, part, order)
    live = jnp.arange(tile_rows.shape[-1]) < tile_counts[0, 0][:, None]
    own_rows = jnp.where(live, tile_rows[0, 0], -1).reshape(-1)
    own_cols = tile_cols.reshape(-1)
    target_rows = lax.dynamic_index_in_dim(out_rows[0, 0], layer, 0, keepdims=False)
    target_cols = lax.dynamic_index_in_dim(out_cols[0, 0], layer, 0, keepdims=False)
    pieces = jnp.concatenate([own_rows, own_cols, target_rows, target_cols])
    meta = jnp.zeros((8, 128), jnp.int32).at[0, : pieces.shape[0]].set(pieces)

    anywhere = pl.BlockSpec(memory_space=pl.ANY)
    landed, panel, meta_all = pl.pallas_call(
        functools.partial(spread_kernel, n_row, n_sub, n_layer),
        out_shape=(
            jax.ShapeDtypeStruct((n_sub, slots, part, order), jnp.float32),
            jax.ShapeDtypeStruct((n_row, slots, n_sub, part, order), jnp.float32),
            jax.ShapeDtypeStruct((total, 8, 128), jnp.int32),
        ),
        in_specs=[anywhere, anywhere],
        out_specs=(anywhere, anywhere, anywhere),
        scratch_shapes=[
            pltpu.SemaphoreType.DMA((n_sub,)),
            pltpu.SemaphoreType.DMA((n_sub,)),
            pltpu.SemaphoreType.DMA((n_row,)),
            pltpu.SemaphoreType.DMA((n_row,)),
            pltpu.SemaphoreType.DMA((total,)),
            pltpu.SemaphoreType.DMA((total,)),
            pltpu.SemaphoreType.DMA((3,)),
        ],
        compiler_params=pltpu.CompilerParams(collective_id=1, has_side_effects=True),
        name="spread",
    )(tiles, meta)
    landed = landed.reshape(n_sub * slots, part, order)
    panel = panel.reshape(n_row * slots, order, order)

    lines = meta_all[:, 0, : 2 * slots + 2 * kept].reshape(n_row, n_sub, -1)
    list_rows = lines[:, :, :slots]
    list_cols = lines[:, :, slots : 2 * slots]
    goal_rows = lines[:, :, 2 * slots : 2 * slots + kept]
    goal_cols = lines[:, :, 2 * slots + kept :]
    bits = jnp.left_shift(1, jnp.arange(kept, dtype=jnp.int32))
    left_rows = list_rows.reshape(n_row, n_sub * slots)
    left_cols = list_cols.reshape(n_row, n_sub * slots)
    right_rows = list_rows.transpose(1, 0, 2).reshape(n_sub, n_row * slots)
    right_cols = list_cols.transpose(1, 0, 2).reshape(n_sub, n_row * slots)
    left_bits = jnp.sum(jnp.where(
        left_rows[:, None, None, :] == goal_rows[:, :, :, None], bits[:, None], 0), axis=2)
    right_bits = jnp.sum(jnp.where(
        right_cols[None, :, :, None] == goal_cols[:, :, None, :], bits, 0), axis=3)
    meets = (
        (right_rows[None, :, :, None] == left_cols[:, None, None, :])
        & (jnp.bitwise_and(left_bits[:, :, None, :], right_bits[:, :, :, None]) != 0)
    )
    away = (jnp.arange(n_sub * slots) // slots)[None, :] != jnp.arange(n_sub)[:, None]
    needed = jnp.any(meets, axis=2) & away
    most = jnp.max(jnp.sum(needed.astype(jnp.int32), axis=-1))
    rounds = (most + ROUND - 1) // ROUND
    my_needed = lax.dynamic_index_in_dim(needed, row, 0, keepdims=False)
    rank = jnp.where(my_needed, running_count(my_needed) - 1, -1)
    slot_ids = jnp.arange(n_sub * slots, dtype=jnp.int32)

    my_left_rows = lax.dynamic_index_in_dim(left_rows, row, 0, keepdims=False)
    my_left_cols = lax.dynamic_index_in_dim(left_cols, row, 0, keepdims=False)
    my_goal_rows, my_goal_cols = target_rows, target_cols
    my_right_rows = lax.dynamic_index_in_dim(right_rows, sub, 0, keepdims=False)
    my_right_cols = lax.dynamic_index_in_dim(right_cols, sub, 0, keepdims=False)
    base = n_row * slots

    def one_round(turn, collective_id):
        places = turn * ROUND + jnp.arange(ROUND, dtype=jnp.int32)
        chosen = rank[:, None, :] == places[None, :, None]
        wanted = jnp.sum(jnp.where(chosen, slot_ids, 0), axis=-1)
        arrived = pl.pallas_call(
            functools.partial(deliver_kernel, n_sub, n_layer),
            out_shape=jax.ShapeDtypeStruct((ROUND, n_sub, part, order), jnp.float32),
            in_specs=[
                pl.BlockSpec(memory_space=pltpu.SMEM),
                pl.BlockSpec(memory_space=pltpu.VMEM),
            ],
            out_specs=anywhere,
            scratch_shapes=[
                pltpu.VMEM((n_sub, ROUND, part, order), jnp.float32),
                pltpu.SemaphoreType.DMA((n_sub,)),
                pltpu.SemaphoreType.DMA((n_sub,)),
                pltpu.SemaphoreType.DMA,
            ],
            compiler_params=pltpu.CompilerParams(
                collective_id=collective_id, has_side_effects=True,
                vmem_limit_bytes=32 * 1024 * 1024),
            name="deliver",
        )(wanted, landed)
        arrived = arrived.reshape(ROUND, order, order)

        my_chosen = lax.dynamic_index_in_dim(chosen, sub, 0, keepdims=False)
        far_rows = jnp.max(jnp.where(my_chosen, my_left_rows, -1), axis=-1)
        far_cols = jnp.max(jnp.where(my_chosen, my_left_cols, -1), axis=-1)
        near_rows = jnp.where(turn == 0, own_rows, -1)
        rows = jnp.concatenate([far_rows, near_rows])
        cols = jnp.concatenate([far_cols, own_cols])
        names = jnp.concatenate([
            jnp.arange(ROUND, dtype=jnp.int32),
            ROUND + row * slots + jnp.arange(slots, dtype=jnp.int32)])
        hits = (
            (rows[None, :, None] == my_goal_rows[:, None, None]) & (rows[None, :, None] >= 0)
            & (cols[None, :, None] == my_right_rows[None, None, :])
            & (my_right_cols[None, None, :] == my_goal_cols[:, None, None])
        )
        partner = jnp.max(
            jnp.where(hits, jnp.arange(base, dtype=jnp.int32), -1), axis=-1)
        flags = partner >= 0
        place = jnp.where(flags, running_count(flags) - 1, -1)
        counts = jnp.sum(flags.astype(jnp.int32), axis=-1)
        codes = names[None, :] * base + partner
        at_place = place[:, None, :] == jnp.arange(n_sub, dtype=jnp.int32)[None, :, None]
        listed = jnp.sum(jnp.where(at_place, codes[:, None, :], 0), axis=-1)
        return pl.pallas_call(
            functools.partial(multiply_kernel, base),
            out_shape=jax.ShapeDtypeStruct((kept, order, order), jnp.float32),
            in_specs=[
                pl.BlockSpec(memory_space=pltpu.SMEM),
                pl.BlockSpec(memory_space=pltpu.SMEM),
                pl.BlockSpec(memory_space=pltpu.VMEM),
                pl.BlockSpec(memory_space=pltpu.VMEM),
            ],
            out_specs=pl.BlockSpec(memory_space=pltpu.VMEM),
            compiler_params=pltpu.CompilerParams(vmem_limit_bytes=32 * 1024 * 1024),
            name="multiply",
        )(counts, listed, arrived, panel)

    summed = one_round(0, 2)

    def more(state):
        turn, unused = state
        return turn < rounds

    def again(state):
        turn, so_far = state
        return turn + 1, so_far + one_round(turn, 3)

    unused, summed = lax.while_loop(more, again, (jnp.int32(1), summed))
    return summed.reshape(1, 1, kept, order, order)


def solution(mesh):
    in_specs = (
        P("row", ("col", "layer"), None, None, None, None),
        P("row", ("col", "layer"), None, None),
        P("row", ("col", "layer"), None, None),
        P("row", ("col", "layer"), None),
        P("row", "col", None, None),
        P("row", "col", None, None),
    )
    out_specs = P("row", ("col", "layer"), None, None, None)
    body = functools.partial(local, mesh.shape["row"], mesh.shape["col"], mesh.shape["layer"])
    return jax.shard_map(body, mesh=mesh, in_specs=in_specs, out_specs=out_specs, check_vma=False)
```

```python
import functools

import jax
import jax.numpy as jnp
from jax import lax
from jax.experimental import pallas as pl
from jax.experimental.pallas import tpu as pltpu
from jax.sharding import PartitionSpec as P

ROUND = 14
MESH = pl.DeviceIdType.MESH


def greet(count, device_of):
    barrier = pltpu.get_barrier_semaphore()

    def step(k, unused):
        pl.semaphore_signal(barrier, inc=1, device_id=device_of(k + 1), device_id_type=MESH)
        return unused

    lax.fori_loop(0, count, step, 0)
    pl.semaphore_wait(barrier, count)


def far_first(k, n_sub):
    return n_sub // 2 + (1 - 2 * ((k + 1) % 2)) * ((k + 1) // 2)


def spread_kernel(
    n_row, n_sub, n_layer, tiles, rows, cols, counts, goal_rows, goal_cols, landed, panel, meta_all,
    meta, send_sem, recv_sem, panel_send, panel_recv, meta_send, meta_recv, local_sem,
):
    row = lax.axis_index("row")
    sub = lax.axis_index("col") * n_layer + lax.axis_index("layer")
    total = n_row * n_sub
    flat = row * n_sub + sub

    def device_at(flat_index):
        band, place = flat_index // n_sub, flat_index % n_sub
        return {"row": band, "col": place // n_layer, "layer": place % n_layer}

    def other(k):
        return device_at(lax.rem(flat + k, total))

    greet(total - 1, other)

    lists, slots = rows.shape
    layers, kept = goal_rows.shape
    meta[...] = jnp.zeros_like(meta)
    live = lax.broadcasted_iota(jnp.int32, (lists, slots), 1) < counts[...]
    meta[0:lists, 0:slots] = jnp.where(live, rows[...], -1)
    meta[lists : 2 * lists, 0:slots] = cols[...]
    meta[2 * lists : 2 * lists + layers, 0:kept] = goal_rows[...]
    meta[2 * lists + layers : 2 * lists + 2 * layers, 0:kept] = goal_cols[...]

    def meta_copy(k):
        return pltpu.make_async_remote_copy(
            src_ref=meta, dst_ref=meta_all.at[flat], send_sem=meta_send.at[k],
            recv_sem=meta_recv.at[k], device_id=other(k), device_id_type=MESH)

    def slice_copy(k):
        place = lax.rem(sub + k, n_sub)
        return pltpu.make_async_remote_copy(
            src_ref=tiles.at[:, place], dst_ref=landed.at[sub], send_sem=send_sem.at[k],
            recv_sem=recv_sem.at[k],
            device_id={"row": row, "col": place // n_layer, "layer": place % n_layer},
            device_id_type=MESH)

    def panel_copy(k):
        return pltpu.make_async_remote_copy(
            src_ref=tiles, dst_ref=panel.at[row], send_sem=panel_send.at[k],
            recv_sem=panel_recv.at[k],
            device_id={"row": lax.rem(row + k, n_row), "col": sub // n_layer,
                       "layer": sub % n_layer},
            device_id_type=MESH)

    def each(count, what):
        def step(k, unused):
            what(k + 1)
            return unused
        lax.fori_loop(0, count, step, 0)

    own_meta = pltpu.make_async_copy(meta, meta_all.at[flat], local_sem.at[0])
    own_slice = pltpu.make_async_copy(tiles.at[:, sub], landed.at[sub], local_sem.at[1])
    own_panel = pltpu.make_async_copy(tiles, panel.at[row], local_sem.at[2])
    each(n_sub - 1, lambda k: slice_copy(far_first(k - 1, n_sub)).start())
    each(total - 1, lambda k: meta_copy(k).start())
    each(n_row - 1, lambda k: panel_copy(k).start())
    own_meta.start()
    own_slice.start()
    own_panel.start()
    own_meta.wait()
    own_slice.wait()
    own_panel.wait()
    each(total - 1, lambda k: meta_copy(k).wait())
    each(n_row - 1, lambda k: panel_copy(k).wait())
    each(n_sub - 1, lambda k: slice_copy(k).wait())


def deliver_kernel(n_sub, n_layer, wanted, landed, arrived, packed, send_sem, recv_sem, local_sem):
    row = lax.axis_index("row")
    sub = lax.axis_index("col") * n_layer + lax.axis_index("layer")

    def device_of(place):
        return {"row": row, "col": place // n_layer, "layer": place % n_layer}

    greet(n_sub - 1, lambda k: device_of(lax.rem(sub + k, n_sub)))

    def pack(place):
        for n in range(ROUND):
            packed[place, n] = landed[wanted[place, n]]

    def send(k):
        place = lax.rem(sub + k, n_sub)
        return pltpu.make_async_remote_copy(
            src_ref=packed.at[place], dst_ref=arrived.at[:, sub], send_sem=send_sem.at[k],
            recv_sem=recv_sem.at[k], device_id=device_of(place), device_id_type=MESH)

    def out_step(k, unused):
        shift = far_first(k, n_sub)
        pack(lax.rem(sub + shift, n_sub))
        send(shift).start()
        return unused

    def wait_step(k, unused):
        send(k + 1).wait()
        return unused

    lax.fori_loop(0, n_sub - 1, out_step, 0)
    pack(sub)
    own = pltpu.make_async_copy(packed.at[sub], arrived.at[:, sub], local_sem)
    own.start()
    own.wait()
    lax.fori_loop(0, n_sub - 1, wait_step, 0)


def multiply_kernel(base, counts, listed, arrived, panel, out):
    order = out.shape[-1]

    def split(value):
        high = value.astype(jnp.bfloat16)
        return high, (value - high.astype(jnp.float32)).astype(jnp.bfloat16)

    def product(left, right):
        left_high, left_low = split(left)
        right_high, right_low = split(right)
        lefts = jnp.concatenate([left_high, left_high, left_low], axis=1)
        rights = jnp.concatenate([right_high, right_low, right_high], axis=0)
        return jnp.dot(lefts, rights, preferred_element_type=jnp.float32)

    for o in range(out.shape[0]):
        def add(m, unused):
            code = listed[o, m]
            left_index = code // base
            right = panel[code % base]

            @pl.when(left_index < ROUND)
            def _():
                out[o] += product(arrived[left_index], right)

            @pl.when(left_index >= ROUND)
            def _():
                out[o] += product(panel[left_index - ROUND], right)

            return unused

        out[o] = jnp.zeros((order, order), jnp.float32)
        lax.fori_loop(0, counts[o], add, 0)


def running_count(flags):
    size = flags.shape[-1]
    upper = (jnp.arange(size)[:, None] <= jnp.arange(size)[None, :]).astype(jnp.bfloat16)
    return jnp.dot(flags.astype(jnp.bfloat16), upper,
                   preferred_element_type=jnp.float32).astype(jnp.int32)


def local(n_row, n_col, n_layer, tile_values, tile_rows, tile_cols, tile_counts, out_rows, out_cols):
    order = tile_values.shape[-1]
    slots = tile_values.shape[2] * tile_values.shape[3]
    kept = out_rows.shape[-1]
    n_sub = n_col * n_layer
    part = order // n_sub
    total = n_row * n_sub
    row = lax.axis_index("row")
    layer = lax.axis_index("layer")
    sub = lax.axis_index("col") * n_layer + layer

    tiles = tile_values.reshape(slots, n_sub, part, order)
    own_cols = tile_cols.reshape(-1)
    lists = tile_rows.shape[2]

    anywhere = pl.BlockSpec(memory_space=pl.ANY)
    landed, panel, meta_all = pl.pallas_call(
        functools.partial(spread_kernel, n_row, n_sub, n_layer),
        out_shape=(
            jax.ShapeDtypeStruct((n_sub, slots, part, order), jnp.float32),
            jax.ShapeDtypeStruct((n_row, slots, n_sub, part, order), jnp.float32),
            jax.ShapeDtypeStruct((total, 8, 128), jnp.int32),
        ),
        in_specs=[anywhere] + [pl.BlockSpec(memory_space=pltpu.VMEM)] * 5,
        out_specs=(anywhere, anywhere, anywhere),
        scratch_shapes=[
            pltpu.VMEM((8, 128), jnp.int32),
            pltpu.SemaphoreType.DMA((n_sub,)),
            pltpu.SemaphoreType.DMA((n_sub,)),
            pltpu.SemaphoreType.DMA((n_row,)),
            pltpu.SemaphoreType.DMA((n_row,)),
            pltpu.SemaphoreType.DMA((total,)),
            pltpu.SemaphoreType.DMA((total,)),
            pltpu.SemaphoreType.DMA((3,)),
        ],
        compiler_params=pltpu.CompilerParams(collective_id=1, has_side_effects=True),
        name="spread",
    )(tiles, tile_rows[0, 0], tile_cols[0, 0], tile_counts.reshape(lists, 1),
      out_rows[0, 0], out_cols[0, 0])
    landed = landed.reshape(n_sub * slots, part, order)
    panel = panel.reshape(n_row * slots, order, order)

    lines = meta_all.reshape(n_row, n_col, n_layer, 8, 128)
    per_list = slots // lists
    list_rows = lines[..., 0:lists, :per_list].reshape(n_row, n_sub, slots)
    list_cols = lines[..., lists : 2 * lists, :per_list].reshape(n_row, n_sub, slots)
    goals = lines[:, :, 0, 2 * lists : 2 * lists + 2 * n_layer, :kept]
    goal_rows = goals[:, :, :n_layer].reshape(n_row, n_sub, kept)
    goal_cols = goals[:, :, n_layer:].reshape(n_row, n_sub, kept)
    live = jnp.arange(per_list) < tile_counts[0, 0][:, None]
    own_rows = jnp.where(live, tile_rows[0, 0], -1).reshape(-1)
    target_rows = lax.dynamic_index_in_dim(out_rows[0, 0], layer, 0, keepdims=False)
    target_cols = lax.dynamic_index_in_dim(out_cols[0, 0], layer, 0, keepdims=False)
    bits = jnp.left_shift(1, jnp.arange(kept, dtype=jnp.int32))
    left_rows = list_rows.reshape(n_row, n_sub * slots)
    left_cols = list_cols.reshape(n_row, n_sub * slots)
    right_rows = list_rows.transpose(1, 0, 2).reshape(n_sub, n_row * slots)
    right_cols = list_cols.transpose(1, 0, 2).reshape(n_sub, n_row * slots)
    left_bits = jnp.sum(jnp.where(
        left_rows[:, None, None, :] == goal_rows[:, :, :, None], bits[:, None], 0), axis=2)
    right_bits = jnp.sum(jnp.where(
        right_cols[None, :, :, None] == goal_cols[:, :, None, :], bits, 0), axis=3)
    meets = (
        (right_rows[None, :, :, None] == left_cols[:, None, None, :])
        & (jnp.bitwise_and(left_bits[:, :, None, :], right_bits[:, :, :, None]) != 0)
    )
    away = (jnp.arange(n_sub * slots) // slots)[None, :] != jnp.arange(n_sub)[:, None]
    needed = jnp.any(meets, axis=2) & away
    most = jnp.max(jnp.sum(needed.astype(jnp.int32), axis=-1))
    rounds = (most + ROUND - 1) // ROUND
    my_needed = lax.dynamic_index_in_dim(needed, row, 0, keepdims=False)
    rank = jnp.where(my_needed, running_count(my_needed) - 1, -1)
    slot_ids = jnp.arange(n_sub * slots, dtype=jnp.int32)

    my_left_rows = lax.dynamic_index_in_dim(left_rows, row, 0, keepdims=False)
    my_left_cols = lax.dynamic_index_in_dim(left_cols, row, 0, keepdims=False)
    my_goal_rows, my_goal_cols = target_rows, target_cols
    my_right_rows = lax.dynamic_index_in_dim(right_rows, sub, 0, keepdims=False)
    my_right_cols = lax.dynamic_index_in_dim(right_cols, sub, 0, keepdims=False)
    base = n_row * slots

    def deliver(turn, collective_id):
        places = turn * ROUND + jnp.arange(ROUND, dtype=jnp.int32)
        chosen = rank[:, None, :] == places[None, :, None]
        wanted = jnp.sum(jnp.where(chosen, slot_ids, 0), axis=-1)
        arrived = pl.pallas_call(
            functools.partial(deliver_kernel, n_sub, n_layer),
            out_shape=jax.ShapeDtypeStruct((ROUND, n_sub, part, order), jnp.float32),
            in_specs=[
                pl.BlockSpec(memory_space=pltpu.SMEM),
                pl.BlockSpec(memory_space=pltpu.VMEM),
            ],
            out_specs=anywhere,
            scratch_shapes=[
                pltpu.VMEM((n_sub, ROUND, part, order), jnp.float32),
                pltpu.SemaphoreType.DMA((n_sub,)),
                pltpu.SemaphoreType.DMA((n_sub,)),
                pltpu.SemaphoreType.DMA,
            ],
            compiler_params=pltpu.CompilerParams(
                collective_id=collective_id, has_side_effects=True,
                vmem_limit_bytes=16 * 1024 * 1024),
            name="deliver",
        )(wanted, landed)
        return arrived.reshape(ROUND, order, order), chosen

    def products(turn, arrived, chosen):
        my_chosen = lax.dynamic_index_in_dim(chosen, sub, 0, keepdims=False)
        far_rows = jnp.max(jnp.where(my_chosen, my_left_rows, -1), axis=-1)
        far_cols = jnp.max(jnp.where(my_chosen, my_left_cols, -1), axis=-1)
        near_rows = jnp.where(turn == 0, own_rows, -1)
        rows = jnp.concatenate([far_rows, near_rows])
        cols = jnp.concatenate([far_cols, own_cols])
        names = jnp.concatenate([
            jnp.arange(ROUND, dtype=jnp.int32),
            ROUND + row * slots + jnp.arange(slots, dtype=jnp.int32)])
        hits = (
            (rows[None, :, None] == my_goal_rows[:, None, None]) & (rows[None, :, None] >= 0)
            & (cols[None, :, None] == my_right_rows[None, None, :])
            & (my_right_cols[None, None, :] == my_goal_cols[:, None, None])
        )
        partner = jnp.max(
            jnp.where(hits, jnp.arange(base, dtype=jnp.int32), -1), axis=-1)
        flags = partner >= 0
        place = jnp.where(flags, running_count(flags) - 1, -1)
        counts = jnp.sum(flags.astype(jnp.int32), axis=-1)
        codes = names[None, :] * base + partner
        at_place = place[:, None, :] == jnp.arange(n_sub, dtype=jnp.int32)[None, :, None]
        listed = jnp.sum(jnp.where(at_place, codes[:, None, :], 0), axis=-1)
        return pl.pallas_call(
            functools.partial(multiply_kernel, base),
            out_shape=jax.ShapeDtypeStruct((kept, order, order), jnp.float32),
            in_specs=[
                pl.BlockSpec(memory_space=pltpu.SMEM),
                pl.BlockSpec(memory_space=pltpu.SMEM),
                pl.BlockSpec(memory_space=pltpu.VMEM),
                pl.BlockSpec(memory_space=pltpu.VMEM),
            ],
            out_specs=pl.BlockSpec(memory_space=pltpu.VMEM),
            compiler_params=pltpu.CompilerParams(vmem_limit_bytes=16 * 1024 * 1024),
            name="multiply",
        )(counts, listed, arrived, panel)

    arrived, chosen = deliver(0, 2)

    def more_rounds():
        def again(state):
            turn, so_far = state
            return turn + 1, so_far + products(turn, *deliver(turn, 3))

        start = (jnp.int32(1), products(0, arrived, chosen))
        return lax.while_loop(lambda state: state[0] < rounds, again, start)[1]

    summed = lax.cond(rounds > 1, more_rounds, lambda: products(0, arrived, chosen))
    return summed.reshape(1, 1, kept, order, order)


def solution(mesh):
    in_specs = (
        P("row", ("col", "layer"), None, None, None, None),
        P("row", ("col", "layer"), None, None),
        P("row", ("col", "layer"), None, None),
        P("row", ("col", "layer"), None),
        P("row", "col", None, None),
        P("row", "col", None, None),
    )
    out_specs = P("row", ("col", "layer"), None, None, None)
    body = functools.partial(local, mesh.shape["row"], mesh.shape["col"], mesh.shape["layer"])
    return jax.shard_map(body, mesh=mesh, in_specs=in_specs, out_specs=out_specs, check_vma=False)
```

```python
import functools

import jax
import jax.numpy as jnp
import numpy as np
from jax import lax
from jax.experimental import pallas as pl
from jax.experimental.pallas import tpu as pltpu
from jax.sharding import PartitionSpec as P

ROUND = 14
MESH = pl.DeviceIdType.MESH


def greet(count, device_of):
    barrier = pltpu.get_barrier_semaphore()

    def step(k, unused):
        pl.semaphore_signal(barrier, inc=1, device_id=device_of(k + 1), device_id_type=MESH)
        return unused

    lax.fori_loop(0, count, step, 0)
    pl.semaphore_wait(barrier, count)


def far_first(k, n_sub):
    return n_sub // 2 + (1 - 2 * ((k + 1) % 2)) * ((k + 1) // 2)


def spread_kernel(
    n_row, n_sub, n_layer, tiles, rows, cols, counts, goal_rows, goal_cols, landed, panel, meta_all,
    meta, send_sem, recv_sem, panel_send, panel_recv, meta_send, meta_recv, local_sem,
):
    row = lax.axis_index("row")
    sub = lax.axis_index("col") * n_layer + lax.axis_index("layer")
    total = n_row * n_sub
    flat = row * n_sub + sub

    def device_at(flat_index):
        band, place = flat_index // n_sub, flat_index % n_sub
        return {"row": band, "col": place // n_layer, "layer": place % n_layer}

    def other(k):
        return device_at(lax.rem(flat + k, total))

    greet(total - 1, other)

    lists, slots = rows.shape
    layers, kept = goal_rows.shape
    meta[...] = jnp.zeros_like(meta)
    slot = lax.broadcasted_iota(jnp.int32, (1, slots), 1)
    for h in range(lists):
        live = slot < counts[0:1, h : h + 1]
        meta[h : h + 1, 0:slots] = jnp.where(live, rows[h : h + 1, :], -1)
    meta[lists : 2 * lists, 0:slots] = cols[...]
    meta[2 * lists : 2 * lists + layers, 0:kept] = goal_rows[...]
    meta[2 * lists + layers : 2 * lists + 2 * layers, 0:kept] = goal_cols[...]

    def meta_copy(k):
        return pltpu.make_async_remote_copy(
            src_ref=meta, dst_ref=meta_all.at[flat], send_sem=meta_send.at[k],
            recv_sem=meta_recv.at[k], device_id=other(k), device_id_type=MESH)

    def slice_copy(k):
        place = lax.rem(sub + k, n_sub)
        return pltpu.make_async_remote_copy(
            src_ref=tiles.at[:, place], dst_ref=landed.at[sub], send_sem=send_sem.at[k],
            recv_sem=recv_sem.at[k],
            device_id={"row": row, "col": place // n_layer, "layer": place % n_layer},
            device_id_type=MESH)

    def panel_copy(k):
        return pltpu.make_async_remote_copy(
            src_ref=tiles, dst_ref=panel.at[row], send_sem=panel_send.at[k],
            recv_sem=panel_recv.at[k],
            device_id={"row": lax.rem(row + k, n_row), "col": sub // n_layer,
                       "layer": sub % n_layer},
            device_id_type=MESH)

    def each(count, what):
        def step(k, unused):
            what(k + 1)
            return unused
        lax.fori_loop(0, count, step, 0)

    own_meta = pltpu.make_async_copy(meta, meta_all.at[flat], local_sem.at[0])
    own_slice = pltpu.make_async_copy(tiles.at[:, sub], landed.at[sub], local_sem.at[1])
    own_panel = pltpu.make_async_copy(tiles, panel.at[row], local_sem.at[2])
    each(total - 1, lambda k: meta_copy(k).start())
    each(n_sub - 1, lambda k: slice_copy(k).start())
    each(n_row - 1, lambda k: panel_copy(k).start())
    own_meta.start()
    own_slice.start()
    own_panel.start()
    own_meta.wait()
    own_slice.wait()
    own_panel.wait()
    each(total - 1, lambda k: meta_copy(k).wait())
    each(n_row - 1, lambda k: panel_copy(k).wait())
    each(n_sub - 1, lambda k: slice_copy(k).wait())


def deliver_kernel(n_sub, n_layer, wanted, landed, arrived, packed, send_sem, recv_sem, local_sem):
    row = lax.axis_index("row")
    sub = lax.axis_index("col") * n_layer + lax.axis_index("layer")

    def device_of(place):
        return {"row": row, "col": place // n_layer, "layer": place % n_layer}

    greet(n_sub - 1, lambda k: device_of(lax.rem(sub + k, n_sub)))

    def pack(place):
        for n in range(ROUND):
            packed[place, n] = landed[wanted[place, n]]

    def send(k):
        place = lax.rem(sub + k, n_sub)
        return pltpu.make_async_remote_copy(
            src_ref=packed.at[place], dst_ref=arrived.at[:, sub], send_sem=send_sem.at[k],
            recv_sem=recv_sem.at[k], device_id=device_of(place), device_id_type=MESH)

    def out_step(k, unused):
        shift = far_first(k, n_sub)
        pack(lax.rem(sub + shift, n_sub))
        send(shift).start()
        return unused

    def wait_step(k, unused):
        send(k + 1).wait()
        return unused

    lax.fori_loop(0, n_sub - 1, out_step, 0)
    pack(sub)
    own = pltpu.make_async_copy(packed.at[sub], arrived.at[:, sub], local_sem)
    own.start()
    own.wait()
    lax.fori_loop(0, n_sub - 1, wait_step, 0)


def multiply_kernel(base, counts, listed, arrived, panel, out):
    order = out.shape[-1]

    def split(value):
        high = value.astype(jnp.bfloat16)
        return high, (value - high.astype(jnp.float32)).astype(jnp.bfloat16)

    def product(left, right):
        left_high, left_low = split(left)
        right_high, right_low = split(right)
        lefts = jnp.concatenate([left_high, left_high, left_low], axis=1)
        rights = jnp.concatenate([right_high, right_low, right_high], axis=0)
        return jnp.dot(lefts, rights, preferred_element_type=jnp.float32)

    for o in range(out.shape[0]):
        def add(m, unused):
            code = listed[o, m]
            left_index = code // base
            right = panel[code % base]

            @pl.when(left_index < ROUND)
            def _():
                out[o] += product(arrived[left_index], right)

            @pl.when(left_index >= ROUND)
            def _():
                out[o] += product(panel[left_index - ROUND], right)

            return unused

        out[o] = jnp.zeros((order, order), jnp.float32)
        lax.fori_loop(0, counts[o], add, 0)


def running_count(flags):
    size = flags.shape[-1]
    upper = jnp.asarray(np.triu(np.ones((size, size), np.float32)), jnp.bfloat16)
    return jnp.dot(flags.astype(jnp.bfloat16), upper,
                   preferred_element_type=jnp.float32).astype(jnp.int32)


def local(n_row, n_col, n_layer, tile_values, tile_rows, tile_cols, tile_counts, out_rows, out_cols):
    order = tile_values.shape[-1]
    slots = tile_values.shape[2] * tile_values.shape[3]
    kept = out_rows.shape[-1]
    n_sub = n_col * n_layer
    part = order // n_sub
    total = n_row * n_sub
    row = lax.axis_index("row")
    layer = lax.axis_index("layer")
    sub = lax.axis_index("col") * n_layer + layer

    tiles = tile_values.reshape(slots, n_sub, part, order)
    lists = tile_rows.shape[2]

    anywhere = pl.BlockSpec(memory_space=pl.ANY)
    landed, panel, meta_all = pl.pallas_call(
        functools.partial(spread_kernel, n_row, n_sub, n_layer),
        out_shape=(
            jax.ShapeDtypeStruct((n_sub, slots, part, order), jnp.float32),
            jax.ShapeDtypeStruct((n_row, slots, n_sub, part, order), jnp.float32),
            jax.ShapeDtypeStruct((total, 8, 128), jnp.int32),
        ),
        in_specs=[anywhere] + [pl.BlockSpec(memory_space=pltpu.VMEM)] * 5,
        out_specs=(anywhere, anywhere, anywhere),
        scratch_shapes=[
            pltpu.VMEM((8, 128), jnp.int32),
            pltpu.SemaphoreType.DMA((n_sub,)),
            pltpu.SemaphoreType.DMA((n_sub,)),
            pltpu.SemaphoreType.DMA((n_row,)),
            pltpu.SemaphoreType.DMA((n_row,)),
            pltpu.SemaphoreType.DMA((total,)),
            pltpu.SemaphoreType.DMA((total,)),
            pltpu.SemaphoreType.DMA((3,)),
        ],
        compiler_params=pltpu.CompilerParams(collective_id=1, has_side_effects=True),
        name="spread",
    )(tiles, tile_rows[0, 0], tile_cols[0, 0], tile_counts[0],
      out_rows[0, 0], out_cols[0, 0])
    landed = landed.reshape(n_sub * slots, part, order)
    panel = panel.reshape(n_row * slots, order, order)

    lines = meta_all.reshape(n_row, n_col, n_layer, 8, 128)
    per_list = slots // lists
    list_rows = lines[..., 0:lists, :per_list].reshape(n_row, n_sub, slots)
    list_cols = lines[..., lists : 2 * lists, :per_list].reshape(n_row, n_sub, slots)
    goals = lines[:, :, 0, 2 * lists : 2 * lists + 2 * n_layer, :kept]
    goal_rows = goals[:, :, :n_layer].reshape(n_row, n_sub, kept)
    goal_cols = goals[:, :, n_layer:].reshape(n_row, n_sub, kept)
    own_rows = list_rows[row, sub]
    own_cols = list_cols[row, sub]
    target_rows = goal_rows[row, sub]
    target_cols = goal_cols[row, sub]
    bits = jnp.left_shift(1, jnp.arange(kept, dtype=jnp.int32))
    left_rows = list_rows.reshape(n_row, n_sub * slots)
    left_cols = list_cols.reshape(n_row, n_sub * slots)
    right_rows = list_rows.transpose(1, 0, 2).reshape(n_sub, n_row * slots)
    right_cols = list_cols.transpose(1, 0, 2).reshape(n_sub, n_row * slots)
    left_bits = jnp.sum(jnp.where(
        left_rows[:, None, None, :] == goal_rows[:, :, :, None], bits[:, None], 0), axis=2)
    right_bits = jnp.sum(jnp.where(
        right_cols[None, :, :, None] == goal_cols[:, :, None, :], bits, 0), axis=3)
    meets = (
        (right_rows[None, :, :, None] == left_cols[:, None, None, :])
        & (jnp.bitwise_and(left_bits[:, :, None, :], right_bits[:, :, :, None]) != 0)
    )
    away = (jnp.arange(n_sub * slots) // slots)[None, :] != jnp.arange(n_sub)[:, None]
    needed = jnp.any(meets, axis=2) & away
    most = jnp.max(jnp.sum(needed.astype(jnp.int32), axis=-1))
    rounds = (most + ROUND - 1) // ROUND
    my_needed = lax.dynamic_index_in_dim(needed, row, 0, keepdims=False)
    rank = jnp.where(my_needed, running_count(my_needed) - 1, -1)
    slot_ids = jnp.arange(n_sub * slots, dtype=jnp.int32)

    my_left_rows = lax.dynamic_index_in_dim(left_rows, row, 0, keepdims=False)
    my_left_cols = lax.dynamic_index_in_dim(left_cols, row, 0, keepdims=False)
    my_goal_rows, my_goal_cols = target_rows, target_cols
    my_right_rows = lax.dynamic_index_in_dim(right_rows, sub, 0, keepdims=False)
    my_right_cols = lax.dynamic_index_in_dim(right_cols, sub, 0, keepdims=False)
    base = n_row * slots

    def deliver(turn, collective_id):
        places = turn * ROUND + jnp.arange(ROUND, dtype=jnp.int32)
        chosen = rank[:, None, :] == places[None, :, None]
        wanted = jnp.sum(jnp.where(chosen, slot_ids, 0), axis=-1)
        arrived = pl.pallas_call(
            functools.partial(deliver_kernel, n_sub, n_layer),
            out_shape=jax.ShapeDtypeStruct((ROUND, n_sub, part, order), jnp.float32),
            in_specs=[
                pl.BlockSpec(memory_space=pltpu.SMEM),
                pl.BlockSpec(memory_space=pltpu.VMEM),
            ],
            out_specs=anywhere,
            scratch_shapes=[
                pltpu.VMEM((n_sub, ROUND, part, order), jnp.float32),
                pltpu.SemaphoreType.DMA((n_sub,)),
                pltpu.SemaphoreType.DMA((n_sub,)),
                pltpu.SemaphoreType.DMA,
            ],
            compiler_params=pltpu.CompilerParams(
                collective_id=collective_id, has_side_effects=True,
                vmem_limit_bytes=32 * 1024 * 1024),
            name="deliver",
        )(wanted, landed)
        return arrived.reshape(ROUND, order, order), chosen

    def products(turn, arrived, chosen):
        my_chosen = lax.dynamic_index_in_dim(chosen, sub, 0, keepdims=False)
        far_rows = jnp.max(jnp.where(my_chosen, my_left_rows, -1), axis=-1)
        far_cols = jnp.max(jnp.where(my_chosen, my_left_cols, -1), axis=-1)
        near_rows = jnp.where(turn == 0, own_rows, -1)
        rows = jnp.concatenate([far_rows, near_rows])
        cols = jnp.concatenate([far_cols, own_cols])
        names = jnp.concatenate([
            jnp.arange(ROUND, dtype=jnp.int32),
            ROUND + row * slots + jnp.arange(slots, dtype=jnp.int32)])
        hits = (
            (rows[None, :, None] == my_goal_rows[:, None, None]) & (rows[None, :, None] >= 0)
            & (cols[None, :, None] == my_right_rows[None, None, :])
            & (my_right_cols[None, None, :] == my_goal_cols[:, None, None])
        )
        partner = jnp.max(
            jnp.where(hits, jnp.arange(base, dtype=jnp.int32), -1), axis=-1)
        flags = partner >= 0
        place = jnp.where(flags, running_count(flags) - 1, -1)
        counts = jnp.sum(flags.astype(jnp.int32), axis=-1)
        codes = names[None, :] * base + partner
        at_place = place[:, None, :] == jnp.arange(n_sub, dtype=jnp.int32)[None, :, None]
        listed = jnp.sum(jnp.where(at_place, codes[:, None, :], 0), axis=-1)
        return pl.pallas_call(
            functools.partial(multiply_kernel, base),
            out_shape=jax.ShapeDtypeStruct((kept, order, order), jnp.float32),
            in_specs=[
                pl.BlockSpec(memory_space=pltpu.SMEM),
                pl.BlockSpec(memory_space=pltpu.SMEM),
                pl.BlockSpec(memory_space=pltpu.VMEM),
                pl.BlockSpec(memory_space=pltpu.VMEM),
            ],
            out_specs=pl.BlockSpec(memory_space=pltpu.VMEM),
            compiler_params=pltpu.CompilerParams(vmem_limit_bytes=32 * 1024 * 1024),
            name="multiply",
        )(counts, listed, arrived, panel)

    arrived, chosen = deliver(0, 2)

    def again(state):
        turn, so_far = state
        return turn + 1, so_far + products(turn, *deliver(turn, 3))

    start = (jnp.int32(1), products(0, arrived, chosen))
    summed = lax.while_loop(lambda state: state[0] < rounds, again, start)[1]
    return summed.reshape(1, 1, kept, order, order)


def solution(mesh):
    in_specs = (
        P("row", ("col", "layer"), None, None, None, None),
        P("row", ("col", "layer"), None, None),
        P("row", ("col", "layer"), None, None),
        P("row", ("col", "layer"), None),
        P("row", "col", None, None),
        P("row", "col", None, None),
    )
    out_specs = P("row", ("col", "layer"), None, None, None)
    body = functools.partial(local, mesh.shape["row"], mesh.shape["col"], mesh.shape["layer"])
    return jax.shard_map(body, mesh=mesh, in_specs=in_specs, out_specs=out_specs, check_vma=False)
```

```python
import functools

import jax
import jax.numpy as jnp
import numpy as np
from jax import lax
from jax.experimental import pallas as pl
from jax.experimental.pallas import tpu as pltpu
from jax.sharding import PartitionSpec as P

ROUND = 14
MESH = pl.DeviceIdType.MESH


def greet(count, device_of):
    barrier = pltpu.get_barrier_semaphore()

    def step(k, unused):
        pl.semaphore_signal(barrier, inc=1, device_id=device_of(k + 1), device_id_type=MESH)
        return unused

    lax.fori_loop(0, count, step, 0)
    pl.semaphore_wait(barrier, count)


def spread_kernel(
    n_row, n_sub, n_layer, tiles, rows, cols, counts, goal_rows, goal_cols, landed, panel, meta_all,
    meta, send_sem, recv_sem, panel_send, panel_recv, meta_send, meta_recv, local_sem,
):
    row = lax.axis_index("row")
    sub = lax.axis_index("col") * n_layer + lax.axis_index("layer")
    total = n_row * n_sub
    flat = row * n_sub + sub

    def device_at(flat_index):
        band, place = flat_index // n_sub, flat_index % n_sub
        return {"row": band, "col": place // n_layer, "layer": place % n_layer}

    def other(k):
        return device_at(lax.rem(flat + k, total))

    greet(total - 1, other)

    lists, slots = rows.shape
    layers, kept = goal_rows.shape
    meta[...] = jnp.zeros_like(meta)
    slot = lax.broadcasted_iota(jnp.int32, (1, slots), 1)
    for h in range(lists):
        live = slot < counts[0:1, h : h + 1]
        meta[:, h * slots : (h + 1) * slots] = jnp.where(live, rows[h : h + 1, :], -1)
        start = (lists + h) * slots
        meta[:, start : start + slots] = cols[h : h + 1, :]
    for at in range(layers):
        start = 2 * lists * slots + at * kept
        meta[:, start : start + kept] = goal_rows[at : at + 1, :]
        start += layers * kept
        meta[:, start : start + kept] = goal_cols[at : at + 1, :]

    def meta_copy(k):
        return pltpu.make_async_remote_copy(
            src_ref=meta, dst_ref=meta_all.at[flat], send_sem=meta_send.at[k],
            recv_sem=meta_recv.at[k], device_id=other(k), device_id_type=MESH)

    def slice_copy(k):
        place = lax.rem(sub + k, n_sub)
        return pltpu.make_async_remote_copy(
            src_ref=tiles.at[:, place], dst_ref=landed.at[sub], send_sem=send_sem.at[k],
            recv_sem=recv_sem.at[k],
            device_id={"row": row, "col": place // n_layer, "layer": place % n_layer},
            device_id_type=MESH)

    def panel_copy(k):
        return pltpu.make_async_remote_copy(
            src_ref=tiles, dst_ref=panel.at[row], send_sem=panel_send.at[k],
            recv_sem=panel_recv.at[k],
            device_id={"row": lax.rem(row + k, n_row), "col": sub // n_layer,
                       "layer": sub % n_layer},
            device_id_type=MESH)

    def each(count, what):
        def step(k, unused):
            what(k + 1)
            return unused
        lax.fori_loop(0, count, step, 0)

    own_meta = pltpu.make_async_copy(meta, meta_all.at[flat], local_sem.at[0])
    own_slice = pltpu.make_async_copy(tiles.at[:, sub], landed.at[sub], local_sem.at[1])
    own_panel = pltpu.make_async_copy(tiles, panel.at[row], local_sem.at[2])
    each(total - 1, lambda k: meta_copy(k).start())
    each(n_sub - 1, lambda k: slice_copy(k).start())
    each(n_row - 1, lambda k: panel_copy(k).start())
    own_meta.start()
    own_slice.start()
    own_panel.start()
    own_meta.wait()
    own_slice.wait()
    own_panel.wait()
    each(total - 1, lambda k: meta_copy(k).wait())
    each(n_row - 1, lambda k: panel_copy(k).wait())
    each(n_sub - 1, lambda k: slice_copy(k).wait())


def deliver_kernel(n_sub, n_layer, wanted, landed, arrived, packed, send_sem, recv_sem, local_sem):
    row = lax.axis_index("row")
    sub = lax.axis_index("col") * n_layer + lax.axis_index("layer")

    def device_of(place):
        return {"row": row, "col": place // n_layer, "layer": place % n_layer}

    greet(n_sub - 1, lambda k: device_of(lax.rem(sub + k, n_sub)))

    def pack(place):
        for n in range(ROUND):
            packed[place, n] = landed[wanted[place, n]]

    def send(k):
        place = lax.rem(sub + k, n_sub)
        return pltpu.make_async_remote_copy(
            src_ref=packed.at[place], dst_ref=arrived.at[:, sub], send_sem=send_sem.at[k],
            recv_sem=recv_sem.at[k], device_id=device_of(place), device_id_type=MESH)

    def out_step(k, unused):
        shift = k + 1
        pack(lax.rem(sub + shift, n_sub))
        send(shift).start()
        return unused

    def wait_step(k, unused):
        send(k + 1).wait()
        return unused

    lax.fori_loop(0, n_sub - 1, out_step, 0)
    pack(sub)
    own = pltpu.make_async_copy(packed.at[sub], arrived.at[:, sub], local_sem)
    own.start()
    own.wait()
    lax.fori_loop(0, n_sub - 1, wait_step, 0)


def multiply_kernel(base, counts, listed, arrived, panel, out):
    order = out.shape[-1]

    def split(value):
        high = value.astype(jnp.bfloat16)
        return high, (value - high.astype(jnp.float32)).astype(jnp.bfloat16)

    def product(left, right):
        left_high, left_low = split(left)
        right_high, right_low = split(right)
        lefts = jnp.concatenate([left_high, left_high, left_low], axis=1)
        rights = jnp.concatenate([right_high, right_low, right_high], axis=0)
        return jnp.dot(lefts, rights, preferred_element_type=jnp.float32)

    for o in range(out.shape[0]):
        def add(m, unused):
            code = listed[o, m]
            left_index = code // base
            right = panel[code % base]

            @pl.when(left_index < ROUND)
            def _():
                out[o] += product(arrived[left_index], right)

            @pl.when(left_index >= ROUND)
            def _():
                out[o] += product(panel[left_index - ROUND], right)

            return unused

        out[o] = jnp.zeros((order, order), jnp.float32)
        lax.fori_loop(0, counts[o], add, 0)


def running_count(flags):
    size = flags.shape[-1]
    upper = jnp.asarray(np.triu(np.ones((size, size), np.float32)), jnp.bfloat16)
    return jnp.dot(flags.astype(jnp.bfloat16), upper,
                   preferred_element_type=jnp.float32).astype(jnp.int32)


def local(n_row, n_col, n_layer, tile_values, tile_rows, tile_cols, tile_counts, out_rows, out_cols):
    order = tile_values.shape[-1]
    slots = tile_values.shape[2] * tile_values.shape[3]
    kept = out_rows.shape[-1]
    n_sub = n_col * n_layer
    part = order // n_sub
    total = n_row * n_sub
    row = lax.axis_index("row")
    layer = lax.axis_index("layer")
    sub = lax.axis_index("col") * n_layer + layer

    tiles = tile_values.reshape(slots, n_sub, part, order)
    lists = tile_rows.shape[2]

    anywhere = pl.BlockSpec(memory_space=pl.ANY)
    landed, panel, meta_all = pl.pallas_call(
        functools.partial(spread_kernel, n_row, n_sub, n_layer),
        out_shape=(
            jax.ShapeDtypeStruct((n_sub, slots, part, order), jnp.float32),
            jax.ShapeDtypeStruct((n_row, slots, n_sub, part, order), jnp.float32),
            jax.ShapeDtypeStruct((total, 1, 128), jnp.int32),
        ),
        in_specs=[anywhere] + [pl.BlockSpec(memory_space=pltpu.VMEM)] * 5,
        out_specs=(anywhere, anywhere, anywhere),
        scratch_shapes=[
            pltpu.VMEM((1, 128), jnp.int32),
            pltpu.SemaphoreType.DMA((n_sub,)),
            pltpu.SemaphoreType.DMA((n_sub,)),
            pltpu.SemaphoreType.DMA((n_row,)),
            pltpu.SemaphoreType.DMA((n_row,)),
            pltpu.SemaphoreType.DMA((total,)),
            pltpu.SemaphoreType.DMA((total,)),
            pltpu.SemaphoreType.DMA((3,)),
        ],
        compiler_params=pltpu.CompilerParams(collective_id=1, has_side_effects=True),
        name="spread",
    )(tiles, tile_rows[0, 0], tile_cols[0, 0], tile_counts[0],
      out_rows[0, 0], out_cols[0, 0])
    landed = landed.reshape(n_sub * slots, part, order)
    panel = panel.reshape(n_row * slots, order, order)

    lines = meta_all.reshape(n_row, n_sub, 128)
    list_rows = lines[:, :, :slots]
    list_cols = lines[:, :, slots : 2 * slots]
    odd = jnp.arange(n_sub)[:, None] % n_layer
    goal_rows, goal_cols = 0, 0
    for at in range(n_layer):
        start = 2 * slots + at * kept
        goal_rows = jnp.where(odd == at, lines[:, :, start : start + kept], goal_rows)
        start += n_layer * kept
        goal_cols = jnp.where(odd == at, lines[:, :, start : start + kept], goal_cols)
    own_rows = list_rows[row, sub]
    own_cols = list_cols[row, sub]
    target_rows = goal_rows[row, sub]
    target_cols = goal_cols[row, sub]
    bits = jnp.left_shift(1, jnp.arange(kept, dtype=jnp.int32))
    left_rows = list_rows.reshape(n_row, n_sub * slots)
    left_cols = list_cols.reshape(n_row, n_sub * slots)
    right_rows = list_rows.transpose(1, 0, 2).reshape(n_sub, n_row * slots)
    right_cols = list_cols.transpose(1, 0, 2).reshape(n_sub, n_row * slots)
    left_bits = jnp.sum(jnp.where(
        left_rows[:, None, None, :] == goal_rows[:, :, :, None], bits[:, None], 0), axis=2)
    right_bits = jnp.sum(jnp.where(
        right_cols[None, :, :, None] == goal_cols[:, :, None, :], bits, 0), axis=3)
    meets = (
        (right_rows[None, :, :, None] == left_cols[:, None, None, :])
        & (jnp.bitwise_and(left_bits[:, :, None, :], right_bits[:, :, :, None]) != 0)
    )
    away = (jnp.arange(n_sub * slots) // slots)[None, :] != jnp.arange(n_sub)[:, None]
    needed = jnp.any(meets, axis=2) & away
    most = jnp.max(jnp.sum(needed.astype(jnp.int32), axis=-1))
    rounds = (most + ROUND - 1) // ROUND
    my_needed = lax.dynamic_index_in_dim(needed, row, 0, keepdims=False)
    rank = jnp.where(my_needed, running_count(my_needed) - 1, -1)
    slot_ids = jnp.arange(n_sub * slots, dtype=jnp.int32)

    my_left_rows = lax.dynamic_index_in_dim(left_rows, row, 0, keepdims=False)
    my_left_cols = lax.dynamic_index_in_dim(left_cols, row, 0, keepdims=False)
    my_goal_rows, my_goal_cols = target_rows, target_cols
    my_right_rows = lax.dynamic_index_in_dim(right_rows, sub, 0, keepdims=False)
    my_right_cols = lax.dynamic_index_in_dim(right_cols, sub, 0, keepdims=False)
    base = n_row * slots

    def deliver(turn, collective_id):
        places = turn * ROUND + jnp.arange(ROUND, dtype=jnp.int32)
        chosen = rank[:, None, :] == places[None, :, None]
        wanted = jnp.sum(jnp.where(chosen, slot_ids, 0), axis=-1)
        arrived = pl.pallas_call(
            functools.partial(deliver_kernel, n_sub, n_layer),
            out_shape=jax.ShapeDtypeStruct((ROUND, n_sub, part, order), jnp.float32),
            in_specs=[
                pl.BlockSpec(memory_space=pltpu.SMEM),
                pl.BlockSpec(memory_space=pltpu.VMEM),
            ],
            out_specs=anywhere,
            scratch_shapes=[
                pltpu.VMEM((n_sub, ROUND, part, order), jnp.float32),
                pltpu.SemaphoreType.DMA((n_sub,)),
                pltpu.SemaphoreType.DMA((n_sub,)),
                pltpu.SemaphoreType.DMA,
            ],
            compiler_params=pltpu.CompilerParams(
                collective_id=collective_id, has_side_effects=True,
                vmem_limit_bytes=32 * 1024 * 1024),
            name="deliver",
        )(wanted, landed)
        return arrived.reshape(ROUND, order, order), chosen

    def products(turn, arrived, chosen):
        my_chosen = lax.dynamic_index_in_dim(chosen, sub, 0, keepdims=False)
        far_rows = jnp.max(jnp.where(my_chosen, my_left_rows, -1), axis=-1)
        far_cols = jnp.max(jnp.where(my_chosen, my_left_cols, -1), axis=-1)
        near_rows = jnp.where(turn == 0, own_rows, -1)
        rows = jnp.concatenate([far_rows, near_rows])
        cols = jnp.concatenate([far_cols, own_cols])
        names = jnp.concatenate([
            jnp.arange(ROUND, dtype=jnp.int32),
            ROUND + row * slots + jnp.arange(slots, dtype=jnp.int32)])
        hits = (
            (rows[None, :, None] == my_goal_rows[:, None, None]) & (rows[None, :, None] >= 0)
            & (cols[None, :, None] == my_right_rows[None, None, :])
            & (my_right_cols[None, None, :] == my_goal_cols[:, None, None])
        )
        partner = jnp.max(
            jnp.where(hits, jnp.arange(base, dtype=jnp.int32), -1), axis=-1)
        flags = partner >= 0
        place = jnp.where(flags, running_count(flags) - 1, -1)
        counts = jnp.sum(flags.astype(jnp.int32), axis=-1)
        codes = names[None, :] * base + partner
        at_place = place[:, None, :] == jnp.arange(n_sub, dtype=jnp.int32)[None, :, None]
        listed = jnp.sum(jnp.where(at_place, codes[:, None, :], 0), axis=-1)
        return pl.pallas_call(
            functools.partial(multiply_kernel, base),
            out_shape=jax.ShapeDtypeStruct((kept, order, order), jnp.float32),
            in_specs=[
                pl.BlockSpec(memory_space=pltpu.SMEM),
                pl.BlockSpec(memory_space=pltpu.SMEM),
                pl.BlockSpec(memory_space=pltpu.VMEM),
                pl.BlockSpec(memory_space=pltpu.VMEM),
            ],
            out_specs=pl.BlockSpec(memory_space=pltpu.VMEM),
            compiler_params=pltpu.CompilerParams(vmem_limit_bytes=32 * 1024 * 1024),
            name="multiply",
        )(counts, listed, arrived, panel)

    arrived, chosen = deliver(0, 2)

    def again(state):
        turn, so_far = state
        return turn + 1, so_far + products(turn, *deliver(turn, 3))

    start = (jnp.int32(1), products(0, arrived, chosen))
    summed = lax.while_loop(lambda state: state[0] < rounds, again, start)[1]
    return summed.reshape(1, 1, kept, order, order)


def solution(mesh):
    in_specs = (
        P("row", ("col", "layer"), None, None, None, None),
        P("row", ("col", "layer"), None, None),
        P("row", ("col", "layer"), None, None),
        P("row", ("col", "layer"), None),
        P("row", "col", None, None),
        P("row", "col", None, None),
    )
    out_specs = P("row", ("col", "layer"), None, None, None)
    body = functools.partial(local, mesh.shape["row"], mesh.shape["col"], mesh.shape["layer"])
    return jax.shard_map(body, mesh=mesh, in_specs=in_specs, out_specs=out_specs, check_vma=False)
```

```python
import functools

import jax
import jax.numpy as jnp
import numpy as np
from jax import lax
from jax.experimental import pallas as pl
from jax.experimental.pallas import tpu as pltpu
from jax.sharding import PartitionSpec as P

ROUND = 14
MESH = pl.DeviceIdType.MESH


def greet(count, device_of):
    barrier = pltpu.get_barrier_semaphore()

    def step(k, unused):
        pl.semaphore_signal(barrier, inc=1, device_id=device_of(k + 1), device_id_type=MESH)
        return unused

    lax.fori_loop(0, count, step, 0)
    pl.semaphore_wait(barrier, count)


def both_ways(k, n_sub):
    return (1 - k % 2) * (1 + k // 2) + (k % 2) * (n_sub - (k + 1) // 2)


def spread_kernel(
    n_row, n_sub, n_layer, tiles, rows, cols, counts, goal_rows, goal_cols, landed, panel, meta_all,
    meta, send_sem, recv_sem, panel_send, panel_recv, meta_send, meta_recv, local_sem,
):
    row = lax.axis_index("row")
    sub = lax.axis_index("col") * n_layer + lax.axis_index("layer")
    total = n_row * n_sub
    flat = row * n_sub + sub

    def device_at(flat_index):
        band, place = flat_index // n_sub, flat_index % n_sub
        return {"row": band, "col": place // n_layer, "layer": place % n_layer}

    def other(k):
        return device_at(lax.rem(flat + k, total))

    greet(total - 1, other)

    lists, slots = rows.shape
    layers, kept = goal_rows.shape
    meta[...] = jnp.zeros_like(meta)
    slot = lax.broadcasted_iota(jnp.int32, (1, slots), 1)
    for h in range(lists):
        live = slot < counts[0:1, h : h + 1]
        meta[:, h * slots : (h + 1) * slots] = jnp.where(live, rows[h : h + 1, :], -1)
        start = (lists + h) * slots
        meta[:, start : start + slots] = cols[h : h + 1, :]
    for at in range(layers):
        start = 2 * lists * slots + at * kept
        meta[:, start : start + kept] = goal_rows[at : at + 1, :]
        start += layers * kept
        meta[:, start : start + kept] = goal_cols[at : at + 1, :]

    def meta_copy(k):
        return pltpu.make_async_remote_copy(
            src_ref=meta, dst_ref=meta_all.at[flat], send_sem=meta_send.at[k],
            recv_sem=meta_recv.at[k], device_id=other(k), device_id_type=MESH)

    def slice_copy(k):
        place = lax.rem(sub + k, n_sub)
        return pltpu.make_async_remote_copy(
            src_ref=tiles.at[:, place], dst_ref=landed.at[sub], send_sem=send_sem.at[k],
            recv_sem=recv_sem.at[k],
            device_id={"row": row, "col": place // n_layer, "layer": place % n_layer},
            device_id_type=MESH)

    def panel_copy(k):
        return pltpu.make_async_remote_copy(
            src_ref=tiles, dst_ref=panel.at[row], send_sem=panel_send.at[k],
            recv_sem=panel_recv.at[k],
            device_id={"row": lax.rem(row + k, n_row), "col": sub // n_layer,
                       "layer": sub % n_layer},
            device_id_type=MESH)

    def each(count, what):
        def step(k, unused):
            what(k + 1)
            return unused
        lax.fori_loop(0, count, step, 0)

    own_meta = pltpu.make_async_copy(meta, meta_all.at[flat], local_sem.at[0])
    own_slice = pltpu.make_async_copy(tiles.at[:, sub], landed.at[sub], local_sem.at[1])
    own_panel = pltpu.make_async_copy(tiles, panel.at[row], local_sem.at[2])
    each(total - 1, lambda k: meta_copy(k).start())
    each(n_sub - 1, lambda k: slice_copy(both_ways(k - 1, n_sub)).start())
    each(n_row - 1, lambda k: panel_copy(k).start())
    own_meta.start()
    own_slice.start()
    own_panel.start()
    own_meta.wait()
    own_slice.wait()
    own_panel.wait()
    each(total - 1, lambda k: meta_copy(k).wait())
    each(n_row - 1, lambda k: panel_copy(k).wait())
    each(n_sub - 1, lambda k: slice_copy(k).wait())


def deliver_kernel(n_sub, n_layer, wanted, landed, arrived, packed, send_sem, recv_sem, local_sem):
    row = lax.axis_index("row")
    sub = lax.axis_index("col") * n_layer + lax.axis_index("layer")

    def device_of(place):
        return {"row": row, "col": place // n_layer, "layer": place % n_layer}

    greet(n_sub - 1, lambda k: device_of(lax.rem(sub + k, n_sub)))

    def pack(place):
        for n in range(ROUND):
            packed[place, n] = landed[wanted[place, n]]

    def send(k):
        place = lax.rem(sub + k, n_sub)
        return pltpu.make_async_remote_copy(
            src_ref=packed.at[place], dst_ref=arrived.at[:, sub], send_sem=send_sem.at[k],
            recv_sem=recv_sem.at[k], device_id=device_of(place), device_id_type=MESH)

    def out_step(k, unused):
        shift = both_ways(k, n_sub)
        pack(lax.rem(sub + shift, n_sub))
        send(shift).start()
        return unused

    def wait_step(k, unused):
        send(k + 1).wait()
        return unused

    lax.fori_loop(0, n_sub - 1, out_step, 0)
    pack(sub)
    own = pltpu.make_async_copy(packed.at[sub], arrived.at[:, sub], local_sem)
    own.start()
    own.wait()
    lax.fori_loop(0, n_sub - 1, wait_step, 0)


def multiply_kernel(base, counts, listed, arrived, panel, out):
    order = out.shape[-1]

    def split(value):
        high = value.astype(jnp.bfloat16)
        return high, (value - high.astype(jnp.float32)).astype(jnp.bfloat16)

    def product(left, right):
        left_high, left_low = split(left)
        right_high, right_low = split(right)
        lefts = jnp.concatenate([left_high, left_high, left_low], axis=1)
        rights = jnp.concatenate([right_high, right_low, right_high], axis=0)
        return jnp.dot(lefts, rights, preferred_element_type=jnp.float32)

    for o in range(out.shape[0]):
        def add(m, unused):
            code = listed[o, m]
            left_index = code // base
            right = panel[code % base]

            @pl.when(left_index < ROUND)
            def _():
                out[o] += product(arrived[left_index], right)

            @pl.when(left_index >= ROUND)
            def _():
                out[o] += product(panel[left_index - ROUND], right)

            return unused

        out[o] = jnp.zeros((order, order), jnp.float32)
        lax.fori_loop(0, counts[o], add, 0)


def running_count(flags):
    size = flags.shape[-1]
    upper = jnp.asarray(np.triu(np.ones((size, size), np.float32)), jnp.bfloat16)
    return jnp.dot(flags.astype(jnp.bfloat16), upper,
                   preferred_element_type=jnp.float32).astype(jnp.int32)


def local(n_row, n_col, n_layer, tile_values, tile_rows, tile_cols, tile_counts, out_rows, out_cols):
    order = tile_values.shape[-1]
    slots = tile_values.shape[2] * tile_values.shape[3]
    kept = out_rows.shape[-1]
    n_sub = n_col * n_layer
    part = order // n_sub
    total = n_row * n_sub
    row = lax.axis_index("row")
    layer = lax.axis_index("layer")
    sub = lax.axis_index("col") * n_layer + layer

    tiles = tile_values.reshape(slots, n_sub, part, order)
    lists = tile_rows.shape[2]

    anywhere = pl.BlockSpec(memory_space=pl.ANY)
    landed, panel, meta_all = pl.pallas_call(
        functools.partial(spread_kernel, n_row, n_sub, n_layer),
        out_shape=(
            jax.ShapeDtypeStruct((n_sub, slots, part, order), jnp.float32),
            jax.ShapeDtypeStruct((n_row, slots, n_sub, part, order), jnp.float32),
            jax.ShapeDtypeStruct((total, 1, 128), jnp.int32),
        ),
        in_specs=[anywhere] + [pl.BlockSpec(memory_space=pltpu.VMEM)] * 5,
        out_specs=(anywhere, anywhere, anywhere),
        scratch_shapes=[
            pltpu.VMEM((1, 128), jnp.int32),
            pltpu.SemaphoreType.DMA((n_sub,)),
            pltpu.SemaphoreType.DMA((n_sub,)),
            pltpu.SemaphoreType.DMA((n_row,)),
            pltpu.SemaphoreType.DMA((n_row,)),
            pltpu.SemaphoreType.DMA((total,)),
            pltpu.SemaphoreType.DMA((total,)),
            pltpu.SemaphoreType.DMA((3,)),
        ],
        compiler_params=pltpu.CompilerParams(collective_id=1, has_side_effects=True),
        name="spread",
    )(tiles, tile_rows[0, 0], tile_cols[0, 0], tile_counts[0],
      out_rows[0, 0], out_cols[0, 0])
    landed = landed.reshape(n_sub * slots, part, order)
    panel = panel.reshape(n_row * slots, order, order)

    lines = meta_all.reshape(n_row, n_sub, 128)
    list_rows = lines[:, :, :slots]
    list_cols = lines[:, :, slots : 2 * slots]
    odd = jnp.arange(n_sub)[:, None] % n_layer
    goal_rows, goal_cols = 0, 0
    for at in range(n_layer):
        start = 2 * slots + at * kept
        goal_rows = jnp.where(odd == at, lines[:, :, start : start + kept], goal_rows)
        start += n_layer * kept
        goal_cols = jnp.where(odd == at, lines[:, :, start : start + kept], goal_cols)
    own_rows = list_rows[row, sub]
    own_cols = list_cols[row, sub]
    target_rows = goal_rows[row, sub]
    target_cols = goal_cols[row, sub]
    bits = jnp.left_shift(1, jnp.arange(kept, dtype=jnp.int32))
    left_rows = list_rows.reshape(n_row, n_sub * slots)
    left_cols = list_cols.reshape(n_row, n_sub * slots)
    right_rows = list_rows.transpose(1, 0, 2).reshape(n_sub, n_row * slots)
    right_cols = list_cols.transpose(1, 0, 2).reshape(n_sub, n_row * slots)
    left_bits = jnp.sum(jnp.where(
        left_rows[:, None, None, :] == goal_rows[:, :, :, None], bits[:, None], 0), axis=2)
    right_bits = jnp.sum(jnp.where(
        right_cols[None, :, :, None] == goal_cols[:, :, None, :], bits, 0), axis=3)
    meets = (
        (right_rows[None, :, :, None] == left_cols[:, None, None, :])
        & (jnp.bitwise_and(left_bits[:, :, None, :], right_bits[:, :, :, None]) != 0)
    )
    away = (jnp.arange(n_sub * slots) // slots)[None, :] != jnp.arange(n_sub)[:, None]
    needed = jnp.any(meets, axis=2) & away
    most = jnp.max(jnp.sum(needed.astype(jnp.int32), axis=-1))
    rounds = (most + ROUND - 1) // ROUND
    my_needed = lax.dynamic_index_in_dim(needed, row, 0, keepdims=False)
    rank = jnp.where(my_needed, running_count(my_needed) - 1, -1)
    slot_ids = jnp.arange(n_sub * slots, dtype=jnp.int32)

    my_left_rows = lax.dynamic_index_in_dim(left_rows, row, 0, keepdims=False)
    my_left_cols = lax.dynamic_index_in_dim(left_cols, row, 0, keepdims=False)
    my_goal_rows, my_goal_cols = target_rows, target_cols
    my_right_rows = lax.dynamic_index_in_dim(right_rows, sub, 0, keepdims=False)
    my_right_cols = lax.dynamic_index_in_dim(right_cols, sub, 0, keepdims=False)
    base = n_row * slots

    def deliver(turn, collective_id):
        places = turn * ROUND + jnp.arange(ROUND, dtype=jnp.int32)
        chosen = rank[:, None, :] == places[None, :, None]
        wanted = jnp.sum(jnp.where(chosen, slot_ids, 0), axis=-1)
        arrived = pl.pallas_call(
            functools.partial(deliver_kernel, n_sub, n_layer),
            out_shape=jax.ShapeDtypeStruct((ROUND, n_sub, part, order), jnp.float32),
            in_specs=[
                pl.BlockSpec(memory_space=pltpu.SMEM),
                pl.BlockSpec(memory_space=pltpu.VMEM),
            ],
            out_specs=anywhere,
            scratch_shapes=[
                pltpu.VMEM((n_sub, ROUND, part, order), jnp.float32),
                pltpu.SemaphoreType.DMA((n_sub,)),
                pltpu.SemaphoreType.DMA((n_sub,)),
                pltpu.SemaphoreType.DMA,
            ],
            compiler_params=pltpu.CompilerParams(
                collective_id=collective_id, has_side_effects=True,
                vmem_limit_bytes=32 * 1024 * 1024),
            name="deliver",
        )(wanted, landed)
        return arrived.reshape(ROUND, order, order), chosen

    def products(turn, arrived, chosen):
        my_chosen = lax.dynamic_index_in_dim(chosen, sub, 0, keepdims=False)
        far_rows = jnp.max(jnp.where(my_chosen, my_left_rows, -1), axis=-1)
        far_cols = jnp.max(jnp.where(my_chosen, my_left_cols, -1), axis=-1)
        near_rows = jnp.where(turn == 0, own_rows, -1)
        rows = jnp.concatenate([far_rows, near_rows])
        cols = jnp.concatenate([far_cols, own_cols])
        names = jnp.concatenate([
            jnp.arange(ROUND, dtype=jnp.int32),
            ROUND + row * slots + jnp.arange(slots, dtype=jnp.int32)])
        hits = (
            (rows[None, :, None] == my_goal_rows[:, None, None]) & (rows[None, :, None] >= 0)
            & (cols[None, :, None] == my_right_rows[None, None, :])
            & (my_right_cols[None, None, :] == my_goal_cols[:, None, None])
        )
        partner = jnp.max(
            jnp.where(hits, jnp.arange(base, dtype=jnp.int32), -1), axis=-1)
        flags = partner >= 0
        place = jnp.where(flags, running_count(flags) - 1, -1)
        counts = jnp.sum(flags.astype(jnp.int32), axis=-1)
        codes = names[None, :] * base + partner
        at_place = place[:, None, :] == jnp.arange(n_sub, dtype=jnp.int32)[None, :, None]
        listed = jnp.sum(jnp.where(at_place, codes[:, None, :], 0), axis=-1)
        return pl.pallas_call(
            functools.partial(multiply_kernel, base),
            out_shape=jax.ShapeDtypeStruct((kept, order, order), jnp.float32),
            in_specs=[
                pl.BlockSpec(memory_space=pltpu.SMEM),
                pl.BlockSpec(memory_space=pltpu.SMEM),
                pl.BlockSpec(memory_space=pltpu.VMEM),
                pl.BlockSpec(memory_space=pltpu.VMEM),
            ],
            out_specs=pl.BlockSpec(memory_space=pltpu.VMEM),
            compiler_params=pltpu.CompilerParams(vmem_limit_bytes=32 * 1024 * 1024),
            name="multiply",
        )(counts, listed, arrived, panel)

    arrived, chosen = deliver(0, 2)

    def again(state):
        turn, so_far = state
        return turn + 1, so_far + products(turn, *deliver(turn, 3))

    start = (jnp.int32(1), products(0, arrived, chosen))
    summed = lax.while_loop(lambda state: state[0] < rounds, again, start)[1]
    return summed.reshape(1, 1, kept, order, order)


def solution(mesh):
    in_specs = (
        P("row", ("col", "layer"), None, None, None, None),
        P("row", ("col", "layer"), None, None),
        P("row", ("col", "layer"), None, None),
        P("row", ("col", "layer"), None),
        P("row", "col", None, None),
        P("row", "col", None, None),
    )
    out_specs = P("row", ("col", "layer"), None, None, None)
    body = functools.partial(local, mesh.shape["row"], mesh.shape["col"], mesh.shape["layer"])
    return jax.shard_map(body, mesh=mesh, in_specs=in_specs, out_specs=out_specs, check_vma=False)
```
